512 devices in a mesh: ctx: 16 (over z_lo, x, core), head: 32 (over z_hi, y).
Axes of the slice: x: 4, y: 8, z: 8 (z_hi: 4, z_lo: 2; z = z_hi * 2 + z_lo), core: 2. Of those that a mesh axis runs over, the one named last changes fastest.
Arguments:
- queries: bfloat16 [16384, 32, 128], P('ctx', 'head'), may hold values from -96 to 96
- key_states: bfloat16 [16384, 8, 128], P(('ctx', 'head')), may hold values from -4 to 4
- value_states: bfloat16 [16384, 8, 128], P(('ctx', 'head')), may hold values from -6 to 6
Outputs:
- attended: bfloat16 [16384, 32, 128], P('ctx', 'head')
The draws below stay inside these ranges and needn't reach their ends.
All inputs are finite; a program needn't handle non-finite values.
Results may differ from the reference program's by a relative error of at most 0.0059.
Values may be sent and summed in bfloat16 or wider, within the bound.
A program may use at most 64 MiB of HBM per device.

```python
import math
import jax
import jax.numpy as jnp
from jax import lax

HEAD_DIM = 128
GROUP = 4
TOK_DEV = 1024
TOKENS = 16384
QHEADS = 32
KVH = 8


def shared_keys(key):
    return jnp.clip(jax.random.normal(key, (TOKENS, KVH, HEAD_DIM), jnp.float32), -4.0, 4.0)


def draw_key_states(key, part):
    base = shared_keys(key)
    return base.astype(jnp.bfloat16)


def draw_queries(key, part):
    key = jax.random.fold_in(key, 5)
    fresh = jnp.clip(jax.random.normal(key, (TOKENS, QHEADS, HEAD_DIM), jnp.float32), -4.0, 4.0)
    return fresh.astype(jnp.bfloat16)


def block_scale(stream_key, dims, cuts, least, largest):
    gain = 1.0
    for position, shards_of in cuts:
        steps = jax.random.uniform(jax.random.fold_in(jax.random.fold_in(stream_key, 6), position), (shards_of,), jnp.float32, least / len(cuts), largest / len(cuts))
        gain = gain * jnp.repeat(jnp.exp(steps), dims[position] // shards_of).reshape((-1,) + (1,) * (len(dims) - 1 - position))
    return gain


def gaussian(own_key, shape, spread, reach, cuts=(), kind=jnp.bfloat16):
    entries = jax.random.normal(own_key, shape, jnp.float32) * spread
    if len(cuts) > 0:
        entries = block_scale(own_key, shape, cuts, -0.22, 0.18) * entries
    return jnp.clip(entries, min=-reach, max=reach).astype(kind)


def setup_inputs(seed: int = 0) -> dict:
    keys = jax.random.split(jax.random.key(seed), 4)
    queries = draw_queries(jax.random.fold_in(keys[3], 71), 0)
    key_states = draw_key_states(jax.random.fold_in(keys[3], 71), 0)
    value_states = gaussian(keys[2], (TOKENS, KVH, HEAD_DIM), 1.0, 6.0, ((0, 512),))
    return {"queries": queries, "key_states": key_states, "value_states": value_states}


def attend_group(query_group, key_rows, value_rows):
    score_scale = 1.0 / math.sqrt(HEAD_DIM)
    key_pos = jnp.arange(TOKENS, dtype=jnp.int32)

    def one_block(block_index):
        start = block_index * TOK_DEV
        query_block = lax.dynamic_slice_in_dim(query_group, start, TOK_DEV, 1)
        scores = jnp.einsum('gqd,kd->gqk', query_block, key_rows) * score_scale
        query_pos = start + jnp.arange(TOK_DEV, dtype=jnp.int32)
        visible = key_pos[None, :] <= query_pos[:, None]
        scores = jnp.where(visible[None], scores, -1e+30)
        row_max = lax.optimization_barrier(jnp.max(scores, axis=-1, keepdims=True))
        weights = jnp.exp(scores - row_max)
        row_total = lax.optimization_barrier(jnp.sum(weights, axis=-1))
        rounded = lax.optimization_barrier(weights.astype(jnp.bfloat16)).astype(jnp.float32)
        mixed = jnp.einsum('gqk,kd->gqd', rounded, value_rows)
        return mixed / row_total[..., None]
    blocks = lax.map(one_block, jnp.arange(TOKENS // TOK_DEV, dtype=jnp.int32))
    return blocks.transpose(1, 0, 2, 3).reshape(GROUP, TOKENS, HEAD_DIM)

def reference(queries, key_states, value_states):
    grouped = queries.astype(jnp.float32).reshape(TOKENS, KVH, GROUP, HEAD_DIM).transpose(1, 2, 0, 3)
    key_heads = key_states.astype(jnp.float32).transpose(1, 0, 2)
    value_heads = value_states.astype(jnp.float32).transpose(1, 0, 2)
    outputs = lax.map(lambda items: attend_group(items[0], items[1], items[2]), (grouped, key_heads, value_heads))
    return outputs.transpose(2, 0, 1, 3).reshape(TOKENS, QHEADS, HEAD_DIM).astype(jnp.bfloat16)
```

```python
import functools
import math

import jax
import jax.numpy as jnp
from jax import lax
from jax.experimental import pallas as pl
from jax.experimental.pallas import tpu as pltpu
from jax.sharding import PartitionSpec as P

MESH = pl.DeviceIdType.MESH
NEG = -1e30
BLOCKS = 16
QT = 256
XP, XM, X2, SIB, UP, SIB_XP, SIB_XM, SIB_X2, Y_X2, SIB_UP, Y = range(11)


def kernel(q_ref, k_ref, v_ref, o_ref, kv, stage, wide, qc, qh, oh, lh, lh_out, m, l, acc,
           ss, rs, p1s, p1r, qsem, osem, lsem):
    c = lax.axis_index("ctx")
    h = lax.axis_index("head")
    z, x, core = c // 8, (c // 2) % 4, c % 2
    group, lane = h // 4, h % 4
    rows = q_ref.shape[0]
    tiles = rows // QT

    def quarter(r):
        return (lane + r) % 2 + 2 * ((lane // 2 + r // 2) % 2)

    def device(x_, z_, core_, lane_):
        return {"ctx": z_ * 8 + x_ * 2 + core_, "head": group * 4 + lane_}

    xp, xm, x2 = (x + 1) % 4, (x + 3) % 4, (x + 2) % 4
    to_xp, to_xm, to_x2 = (device(t, z, core, lane) for t in (xp, xm, x2))
    to_sib = device(x, z, 1 - core, lane)
    to_z = device(x, 1 - z, core, lane)
    to_mirror = device(3 - x, 1 - z, 1 - core, lane)
    to_y = [None] + [device(x, z, core, quarter(r)) for r in (1, 2, 3)]
    to_group = [None] + [{"ctx": c, "head": ((group + d) % 8) * 4 + lane} for d in range(1, 8)]

    barrier = pltpu.get_barrier_semaphore()
    partners = to_group[1:] + to_y[1:] + [to_xp, to_xm, to_x2, to_sib, to_z, to_mirror]
    for partner in partners:
        pl.semaphore_signal(barrier, inc=1, device_id=partner, device_id_type=MESH)

    for ref, first in ((k_ref, 0), (v_ref, 32)):
        wide[...] = ref[...].astype(jnp.float32).reshape(wide.shape)
        for g in range(8):
            stage[g, first:first + 32] = wide[pl.ds(g, 32, stride=8), :].astype(jnp.bfloat16)
    kv[c, lane, group] = stage[group]

    scale = math.log2(math.e) / math.sqrt(q_ref.shape[1])

    def split_scaled(job, src):
        def one(i, _):
            r = pl.ds(pl.multiple_of(i * QT, QT), QT)
            scaled = src[r].astype(jnp.float32) * scale
            high = scaled.astype(jnp.bfloat16)
            qc[job, r, :128] = high
            qc[job, r, 128:] = (scaled - high.astype(jnp.float32)).astype(jnp.bfloat16)
            return 0
        lax.fori_loop(0, tiles, one, 0)

    split_scaled(0, q_ref)
    m[...] = jnp.full(m.shape, NEG, jnp.float32)
    l[...] = jnp.zeros(l.shape, jnp.float32)
    acc[...] = jnp.zeros(acc.shape, jnp.float32)

    pl.semaphore_wait(barrier, len(partners))

    def remote(src, dst, send, recv, to):
        return pltpu.make_async_remote_copy(
            src_ref=src, dst_ref=dst, send_sem=send, recv_sem=recv, device_id=to, device_id_type=MESH)

    def scatter(d):
        return remote(stage.at[(group + d) % 8], kv.at[c, lane, group], p1s.at[d], p1r.at[d], to_group[d])

    for d in (4, 3, 5, 2, 6, 1, 7):
        scatter(d).start()
    query_copy = remote(q_ref, qh, qsem.at[0], qsem.at[1], to_mirror)

    @pl.when(z == 1)
    def _():
        query_copy.start()

    def piece(kind, r, block, to):
        q = quarter(r)
        return remote(kv.at[block, q], kv.at[block, q], ss.at[kind, r], rs.at[block, q], to)

    def landed(r, block):
        piece(0, r, block, to_sib).wait_recv()

    def from_chip(x_):
        return 2 * x_ + 8 * z * (x_ < x).astype(jnp.int32)

    is_late = z == 1
    own_up = 2 * x + core
    own_goes = {XP: (z == 0) | (x < 3), XM: (z == 0) | (x < 1), X2: (z == 0) | (x < 2)}
    targets = {XP: to_xp, XM: to_xm, X2: to_x2}

    def kinds_x(r_even):
        return (XP, XM, X2) if r_even else (XP, XM)

    def own_quarter(r, r_even, first=False):
        if not first:
            landed(r, c)
        for kind in kinds_x(r_even):
            @pl.when(own_goes[kind])
            def _(kind=kind):
                piece(kind, r, c, targets[kind]).start()

        @pl.when(z == 0)
        def _():
            piece(UP, r, c, to_z).start()

        piece(SIB, r, c, to_sib).start()

    def up_quarter(r, r_even):
        @pl.when(is_late)
        def _():
            landed(r, own_up)
            for kind in kinds_x(r_even):
                @pl.when(jnp.logical_not(own_goes[kind]))
                def _(kind=kind):
                    piece(kind, r, own_up, targets[kind]).start()
            piece(SIB_UP, r, own_up, to_sib).start()

    def x_quarters(r):
        for kind, source in ((SIB_XP, xp), (SIB_XM, xm)):
            landed(r, from_chip(source) + core)
            piece(kind, r, from_chip(source) + core, to_sib).start()

    def x2_quarter(r, r_even):
        block = from_chip(x2) + core
        landed(r, block)
        if r_even:
            piece(Y_X2, r, block, to_y[1]).start()
        piece(SIB_X2, r, block, to_sib).start()

    def sib_near(r):
        landed(r, c + 1 - 2 * core)

        @pl.when(is_late)
        def _():
            landed(r, own_up + 1 - 2 * core)
        landed(r, from_chip(xp) + 1 - core)
        landed(r, from_chip(xm) + 1 - core)

    def sib_far(r):
        landed(r, from_chip(x2) + 1 - core)

    def attend(job, tile, keys, values, mask=None):
        at = slice(tile * QT, (tile + 1) * QT)
        scores = lax.dot_general(qc[job, at], jnp.concatenate([keys, keys], axis=1),
                                 (((1,), (1,)), ((), ())), preferred_element_type=jnp.float32)
        if mask is not None:
            scores = jnp.where(mask, scores, NEG)
        before = m[job, at]
        now = jnp.maximum(before, jnp.max(scores, axis=1, keepdims=True))
        shrink = jnp.exp2(before - now)
        weights = jnp.exp2(scores - now[:, :1]).astype(jnp.bfloat16)
        mixed = jnp.dot(weights, jnp.concatenate([values, jnp.ones_like(values)], axis=1),
                        preferred_element_type=jnp.float32)
        m[job, at] = now
        acc[job, at] = acc[job, at] * shrink + mixed[:, :128]
        l[job, at] = l[job, at] * shrink + mixed[:, 128:]

    def load(blocks, half, first, count):
        parts = [(b, quarter(2 * half + i)) for b in blocks for i in range(2)]
        def side(at):
            return jnp.concatenate(
                [kv[b, q, pl.ds(first, count), at:at + 32, :].reshape(count * 32, 128) for b, q in parts], axis=0)
        return side(0), side(32)

    def diagonal(half):
        for tile in range(tiles):
            count = 2 * (tile + 1)
            keys, values = load([c], half, 0, count)
            spot = lax.broadcasted_iota(jnp.int32, (1, count * 64), 1)
            which = jnp.where(spot < count * 32, quarter(2 * half), quarter(2 * half + 1))
            inner = spot % (count * 32)
            key_pos = (inner // 32) * 128 + which * 32 + inner % 32
            query_pos = tile * QT + lax.broadcasted_iota(jnp.int32, (QT, 1), 0)
            attend(0, tile, keys, values, key_pos <= query_pos)

    def single_and_half(half):
        early = 1 - z
        block = jnp.where(is_late, 2 * x + jnp.where(core == 0, 1, 8), jnp.where(core == 0, 6 - 2 * x, 2 * x))
        job = jnp.where(core == 0, early, 0)
        keys, values = load([block], half, 0, 8)
        for tile in range(tiles):
            attend(job, tile, keys, values)
        block = jnp.where(is_late, 2 * x + core, 7 - 2 * x - core)
        keys, values = load([block], half, 4 * z, 4)
        for tile in range(tiles):
            attend(early, tile, keys, values)

    def by_x(a0, a1, a2, a3):
        return jnp.where(x == 0, a0, jnp.where(x == 1, a1, jnp.where(x == 2, a2, a3)))

    def by_step(i, a0, a1, a2):
        return jnp.where(i == 0, a0, jnp.where(i == 1, a1, a2))

    def pair(i, half):
        late_chip = by_step(i, xp, xm, x2)
        early_chip = by_step(i, by_x(0, 1, 1, 0), by_x(1, 0, 0, 2), by_x(2, 0, 0, 1))
        early_job = by_step(i, by_x(1, 1, 0, 0), by_x(1, 0, 0, 0), by_x(1, 1, 1, 0))
        base = from_chip(jnp.where(is_late, late_chip, early_chip))
        job = jnp.where(is_late, 0, early_job)
        keys, values = load([base, base + 1], half, 0, 8)
        for tile in range(tiles):
            attend(job, tile, keys, values)

    for d in range(1, 8):
        scatter(d).wait_recv()
    for step in (1, 2, 3):
        piece_y = remote(kv.at[c, lane], kv.at[c, lane], ss.at[Y, step], rs.at[c, lane], to_y[step])
        piece_y.start()
    own_quarter(0, True, True)
    up_quarter(0, True)
    x_quarters(0)
    own_quarter(1, False)

    @pl.when(z == 0)
    def _():
        query_copy.wait_recv()
        split_scaled(1, qh)

    def both(half, _):
        first = half == 0
        r0, r1 = 2 * half, 2 * half + 1
        diagonal(half)

        @pl.when(first)
        def _():
            x2_quarter(0, True)
        up_quarter(r1, False)
        x_quarters(r1)

        @pl.when(first)
        def _():
            own_quarter(2, True)
        sib_near(r0)
        sib_near(r1)
        single_and_half(half)

        @pl.when(first)
        def _():
            own_quarter(3, False)
            up_quarter(2, True)
            x_quarters(2)

        def one(i, _):
            @pl.when(i == 1)
            def _():
                x2_quarter(r1, False)
                sib_far(r0)
                sib_far(r1)

            pair(i, half)

            @pl.when((i == 1) & first)
            def _():
                x2_quarter(2, True)
            return 0
        lax.fori_loop(0, 3, one, 0)
        return 0

    lax.fori_loop(0, 2, both, 0)

    eye = (lax.broadcasted_iota(jnp.int32, (128, 128), 0) == lax.broadcasted_iota(jnp.int32, (128, 128), 1))
    out_copy = remote(oh, qh, osem.at[0], osem.at[1], to_mirror)
    log_copy = remote(lh_out, lh, lsem.at[0], lsem.at[1], to_mirror)

    @pl.when(z == 0)
    def _():
        for i in range(rows // 128):
            at = slice(i * 128, (i + 1) * 128)
            oh[at] = (acc[1, at] / l[1, at]).astype(jnp.bfloat16)
            log = m[1, at] + jnp.log2(l[1, at])
            lh_out[i:i + 1] = jnp.sum(jnp.where(eye, log, 0.0), axis=0, keepdims=True)
        log_copy.start()
        out_copy.start()
        o_ref[...] = (acc[0] / l[0]).astype(jnp.bfloat16)

    @pl.when(z == 1)
    def _():
        query_copy.wait_send()
        log_copy.wait_recv()
        out_copy.wait_recv()
        for i in range(rows // 128):
            at = slice(i * 128, (i + 1) * 128)
            log = jnp.sum(jnp.where(eye, lh[i:i + 1], 0.0), axis=1, keepdims=True)
            mine = m[0, at]
            top = jnp.maximum(mine, log)
            w_mine, w_help = jnp.exp2(mine - top), jnp.exp2(log - top)
            total = l[0, at] * w_mine + w_help
            mixed = acc[0, at] * w_mine + qh[at].astype(jnp.float32) * w_help
            o_ref[at] = (mixed / total).astype(jnp.bfloat16)

    @pl.when(z == 0)
    def _():
        log_copy.wait_send()
        out_copy.wait_send()
    for d in range(1, 8):
        scatter(d).wait_send()
    for r in range(4):
        kinds = [XP, XM, SIB, SIB_XP, SIB_XM, SIB_X2] + ([X2, Y_X2] if r % 2 == 0 else []) + ([Y] if r else [])
        for kind in kinds:
            piece(kind, r, c, to_sib).wait_send()
        for kind, when in ((UP, z == 0), (SIB_UP, z == 1)):
            @pl.when(when)
            def _(kind=kind):
                piece(kind, r, c, to_sib).wait_send()


def per_device(queries, key_states, value_states):
    rows, _, width = queries.shape
    f32, bf16 = jnp.float32, jnp.bfloat16
    dma = pltpu.SemaphoreType.DMA
    out = pl.pallas_call(
        kernel,
        out_shape=jax.ShapeDtypeStruct((rows, width), bf16),
        in_specs=[pl.BlockSpec(memory_space=pltpu.VMEM)] * 3,
        out_specs=pl.BlockSpec(memory_space=pltpu.VMEM),
        scratch_shapes=[
            pltpu.VMEM((BLOCKS, 4, 8, 64, width), bf16),
            pltpu.VMEM((8, 64, width), bf16),
            pltpu.VMEM((256, width), f32),
            pltpu.VMEM((2, rows, 2 * width), bf16),
            pltpu.VMEM((rows, width), bf16),
            pltpu.VMEM((rows, width), bf16),
            pltpu.VMEM((8, 128), f32),
            pltpu.VMEM((8, 128), f32),
            pltpu.VMEM((2, rows, width), f32),
            pltpu.VMEM((2, rows, width), f32),
            pltpu.VMEM((2, rows, width), f32),
            dma((11, 4)),
            dma((BLOCKS, 4)),
            dma((8,)),
            dma((8,)),
            dma((2,)),
            dma((2,)),
            dma((2,)),
        ],
        name="folded_attention",
        cost_estimate=pl.CostEstimate(flops=4 * 128 * 8 * 1024 * 1024, bytes_accessed=2**20, transcendentals=2**23),
        compiler_params=pltpu.CompilerParams(
            collective_id=0, has_side_effects=True, vmem_limit_bytes=48 * 2**20),
    )(queries.reshape(rows, width), key_states, value_states)
    return out[:, None, :]


def solution(mesh):
    return jax.shard_map(
        per_device,
        mesh=mesh,
        in_specs=(
            P("ctx", "head", None),
            P(("ctx", "head"), None, None),
            P(("ctx", "head"), None, None),
        ),
        out_specs=P("ctx", "head", None),
        check_vma=False,
    )
```

```python
import functools
import math

import jax
import jax.numpy as jnp
from jax import lax
from jax.experimental import pallas as pl
from jax.experimental.pallas import tpu as pltpu
from jax.sharding import PartitionSpec as P

MESH = pl.DeviceIdType.MESH
NEG = -1e30
BLOCKS = 16
QT = 256
XP, XM, X2, SIB, UP, SIB_XP, SIB_XM, SIB_X2, Y_X2, SIB_UP, Y = range(11)


def kernel(q_hbm, k_hbm, v_hbm, o_ref, q_ref, k_ref, v_ref, kv, stage, wide, qc, qh, oh, lh, lh_out, m, l, acc,
           ss, rs, p1s, p1r, qsem, osem, lsem, isem):
    c = lax.axis_index("ctx")
    h = lax.axis_index("head")
    z, x, core = c // 8, (c // 2) % 4, c % 2
    group, lane = h // 4, h % 4
    rows = q_ref.shape[0]
    tiles = rows // QT

    def quarter(r):
        return (lane + r) % 2 + 2 * ((lane // 2 + r // 2) % 2)

    def device(x_, z_, core_, lane_):
        return {"ctx": z_ * 8 + x_ * 2 + core_, "head": group * 4 + lane_}

    xp, xm, x2 = (x + 1) % 4, (x + 3) % 4, (x + 2) % 4
    to_xp, to_xm, to_x2 = (device(t, z, core, lane) for t in (xp, xm, x2))
    to_sib = device(x, z, 1 - core, lane)
    to_z = device(x, 1 - z, core, lane)
    to_mirror = device(3 - x, 1 - z, 1 - core, lane)
    to_y = [None] + [device(x, z, core, quarter(r)) for r in (1, 2, 3)]
    to_group = [None] + [{"ctx": c, "head": ((group + d) % 8) * 4 + lane} for d in range(1, 8)]

    barrier = pltpu.get_barrier_semaphore()
    partners = to_group[1:] + to_y[1:] + [to_xp, to_xm, to_x2, to_sib, to_z, to_mirror]
    for partner in partners:
        pl.semaphore_signal(barrier, inc=1, device_id=partner, device_id_type=MESH)

    loads = [pltpu.make_async_copy(src, dst, isem.at[i])
             for i, (src, dst) in enumerate(((k_hbm, k_ref), (v_hbm, v_ref), (q_hbm, q_ref)))]
    for copy in loads:
        copy.start()
    loads[0].wait()
    loads[1].wait()

    for ref, first in ((k_ref, 0), (v_ref, 32)):
        wide[...] = ref[...].astype(jnp.float32).reshape(wide.shape)
        for g in range(8):
            stage[g, first:first + 32] = wide[pl.ds(g, 32, stride=8), :].astype(jnp.bfloat16)
    kv[c, lane, group] = stage[group]

    scale = math.log2(math.e) / math.sqrt(q_ref.shape[1])

    def split_scaled(job, src):
        def one(i, _):
            r = pl.ds(pl.multiple_of(i * QT, QT), QT)
            scaled = src[r].astype(jnp.float32) * scale
            high = scaled.astype(jnp.bfloat16)
            qc[job, r, :128] = high
            qc[job, r, 128:] = (scaled - high.astype(jnp.float32)).astype(jnp.bfloat16)
            return 0
        lax.fori_loop(0, tiles, one, 0)

    loads[2].wait()
    split_scaled(0, q_ref)
    m[...] = jnp.full(m.shape, NEG, jnp.float32)
    l[...] = jnp.zeros(l.shape, jnp.float32)
    acc[...] = jnp.zeros(acc.shape, jnp.float32)

    pl.semaphore_wait(barrier, len(partners))

    def remote(src, dst, send, recv, to):
        return pltpu.make_async_remote_copy(
            src_ref=src, dst_ref=dst, send_sem=send, recv_sem=recv, device_id=to, device_id_type=MESH)

    def scatter(d):
        return remote(stage.at[(group + d) % 8], kv.at[c, lane, group], p1s.at[d], p1r.at[d], to_group[d])

    for d in (4, 3, 5, 2, 6, 1, 7):
        scatter(d).start()
    query_copy = remote(q_ref, qh, qsem.at[0], qsem.at[1], to_mirror)

    @pl.when(z == 1)
    def _():
        query_copy.start()

    def piece(kind, r, block, to):
        q = quarter(r)
        return remote(kv.at[block, q], kv.at[block, q], ss.at[kind, r], rs.at[block, q], to)

    def landed(r, block):
        piece(0, r, block, to_sib).wait_recv()

    def from_chip(x_):
        return 2 * x_ + 8 * z * (x_ < x).astype(jnp.int32)

    is_late = z == 1
    own_up = 2 * x + core
    own_goes = {XP: (z == 0) | (x < 3), XM: (z == 0) | (x < 1), X2: (z == 0) | (x < 2)}
    targets = {XP: to_xp, XM: to_xm, X2: to_x2}

    def kinds_x(r_even):
        return (XP, XM, X2) if r_even else (XP, XM)

    def own_quarter(r, r_even, first=False):
        if not first:
            landed(r, c)
        @pl.when(z == 0)
        def _():
            piece(UP, r, c, to_z).start()

        for kind in kinds_x(r_even):
            @pl.when(own_goes[kind])
            def _(kind=kind):
                piece(kind, r, c, targets[kind]).start()

        piece(SIB, r, c, to_sib).start()

    def up_quarter(r, r_even):
        @pl.when(is_late)
        def _():
            landed(r, own_up)
            for kind in kinds_x(r_even):
                @pl.when(jnp.logical_not(own_goes[kind]))
                def _(kind=kind):
                    piece(kind, r, own_up, targets[kind]).start()
            piece(SIB_UP, r, own_up, to_sib).start()

    def x_quarters(r):
        for kind, source in ((SIB_XP, xp), (SIB_XM, xm)):
            landed(r, from_chip(source) + core)
            piece(kind, r, from_chip(source) + core, to_sib).start()

    def x2_quarter(r, r_even):
        block = from_chip(x2) + core
        landed(r, block)
        if r_even:
            piece(Y_X2, r, block, to_y[1]).start()
        piece(SIB_X2, r, block, to_sib).start()

    def sib_own(r):
        landed(r, c + 1 - 2 * core)

    def sib_up(r):
        landed(r, own_up + 1 - 2 * core)

    def sib_x(r):
        landed(r, from_chip(xp) + 1 - core)
        landed(r, from_chip(xm) + 1 - core)

    def sib_x2(r):
        landed(r, from_chip(x2) + 1 - core)

    def attend(job, parts):
        scores = []
        for tile, (keys, values, mask) in enumerate(parts):
            at = slice(tile * QT, (tile + 1) * QT)
            score = lax.dot_general(qc[job, at], jnp.concatenate([keys, keys], axis=1),
                                    (((1,), (1,)), ((), ())), preferred_element_type=jnp.float32)
            scores.append(score if mask is None else jnp.where(mask, score, NEG))
        rounded, shrinks = [], []
        for tile, score in enumerate(scores):
            at = slice(tile * QT, (tile + 1) * QT)
            before = m[job, at]
            now = jnp.maximum(before, jnp.max(score, axis=1, keepdims=True))
            m[job, at] = now
            shrinks.append(jnp.exp2(before - now))
            across = jnp.concatenate([now] * (score.shape[1] // 128), axis=1)
            rounded.append(jnp.exp2(score - across).astype(jnp.bfloat16))
        for tile, (_, values, _) in enumerate(parts):
            at = slice(tile * QT, (tile + 1) * QT)
            mixed = jnp.dot(rounded[tile], jnp.concatenate([values, jnp.ones_like(values)], axis=1),
                            preferred_element_type=jnp.float32)
            acc[job, at] = acc[job, at] * shrinks[tile] + mixed[:, :128]
            l[job, at] = l[job, at] * shrinks[tile] + mixed[:, 128:]

    def load(blocks, half, first, count):
        parts = [(b, quarter(2 * half + i)) for b in blocks for i in range(2)]
        def side(at):
            return jnp.concatenate(
                [kv[b, q, pl.ds(first, count), at:at + 32, :].reshape(count * 32, 128) for b, q in parts], axis=0)
        return side(0), side(32)

    def diagonal(half):
        parts = []
        for tile in range(tiles):
            count = 2 * (tile + 1)
            keys, values = load([c], half, 0, count)
            spot = lax.broadcasted_iota(jnp.int32, (1, count * 64), 1)
            which = jnp.where(spot < count * 32, quarter(2 * half), quarter(2 * half + 1))
            inner = spot % (count * 32)
            key_pos = (inner // 32) * 128 + which * 32 + inner % 32
            query_pos = tile * QT + lax.broadcasted_iota(jnp.int32, (QT, 1), 0)
            parts.append((keys, values, key_pos <= query_pos))
        attend(0, parts)

    def single(half):
        keys, values = load([jnp.where(core == 0, 6 - 2 * x, 2 * x)], half, 0, 8)
        attend(1 - core, [(keys, values, None)] * tiles)

    def by_x(a0, a1, a2, a3):
        return jnp.where(x == 0, a0, jnp.where(x == 1, a1, jnp.where(x == 2, a2, a3)))

    def by_step(i, a0, a1, a2):
        return jnp.where(i == 0, a0, jnp.where(i == 1, a1, a2))

    def pair(i, half):
        late_base = from_chip(by_step(i - 1, xp, xm, x2))
        late_a = jnp.where(i == 0, own_up, late_base)
        late_b = jnp.where(i == 0, 2 * x + jnp.where(core == 0, 1, 8), late_base + 1)
        chip_a = by_step(i - 1, by_x(0, 1, 1, 0), by_x(1, 0, 0, 2), by_x(2, 0, 0, 1))
        job_a = by_step(i - 1, by_x(1, 1, 0, 0), by_x(1, 0, 0, 0), by_x(1, 1, 1, 0))
        chip_b = by_step(i - 1, by_x(0, 1, 0, 0), by_x(1, 0, 1, 2), by_x(2, 0, 0, 1))
        job_b = by_step(i - 1, by_x(1, 1, 1, 0), by_x(1, 1, 0, 0), by_x(1, 0, 0, 0))
        early_a = 2 * jnp.where(half == 0, chip_a, chip_b)
        job = jnp.where(is_late, 0, jnp.where(half == 0, job_a, job_b))
        blocks = [jnp.where(is_late, late_a, early_a), jnp.where(is_late, late_b, early_a + 1)]
        keys, values = load(blocks, half, 0, 8)
        attend(job, [(keys, values, None)] * tiles)

    for d in range(1, 8):
        scatter(d).wait_recv()
    for step in (1, 2, 3):
        piece_y = remote(kv.at[c, lane], kv.at[c, lane], ss.at[Y, step], rs.at[c, lane], to_y[step])
        piece_y.start()
    own_quarter(0, True, True)

    @pl.when(z == 0)
    def _():
        query_copy.wait_recv()
        split_scaled(1, qh)

    up_quarter(0, True)
    x_quarters(0)
    own_quarter(1, False)

    eye = (lax.broadcasted_iota(jnp.int32, (128, 128), 0) == lax.broadcasted_iota(jnp.int32, (128, 128), 1))
    out_copy = remote(oh, qh, osem.at[0], osem.at[1], to_mirror)
    log_copy = remote(lh_out, lh, lsem.at[0], lsem.at[1], to_mirror)
    is_early = z == 0

    def send_help():
        for i in range(rows // 128):
            at = slice(i * 128, (i + 1) * 128)
            total = jnp.maximum(l[1, at], 1e-30)
            oh[at] = (acc[1, at] / total).astype(jnp.bfloat16)
            log = m[1, at] + jnp.log2(total)
            lh_out[i:i + 1] = jnp.sum(jnp.where(eye, log, 0.0), axis=0, keepdims=True)
        log_copy.start()
        out_copy.start()

    def both(half, _):
        first = half == 0
        r0, r1 = 2 * half, 2 * half + 1
        diagonal(half)

        @pl.when(first)
        def _():
            own_quarter(2, True)
            x2_quarter(0, True)
            own_quarter(3, False)
            up_quarter(1, False)

        sib_own(r0)
        sib_own(r1)

        def one(i, _):
            @pl.when(is_late & (i == 0))
            def _():
                sib_up(r0)
                sib_up(r1)

            @pl.when((is_early & (i == 0)) | (is_late & (i == 1)))
            def _():
                @pl.when(first)
                def _():
                    x_quarters(1)
                sib_x(r0)
                sib_x(r1)

            @pl.when(first & (i == 1))
            def _():
                up_quarter(2, True)
                up_quarter(3, False)

            @pl.when(first & (i == 2))
            def _():
                x2_quarter(1, False)
                x_quarters(2)

            @pl.when(jnp.where(is_early & (half == 1), i == 0, i == 2))
            def _():
                sib_x2(r0)
                sib_x2(r1)

            @pl.when(first & (i == 3))
            def _():
                x2_quarter(2, True)
                x_quarters(3)

            @pl.when(is_early & (i == 0))
            def _():
                single(half)

            @pl.when(is_late | (i > 0))
            def _():
                pair(i, half)

            @pl.when(first & (i == 3))
            def _():
                x2_quarter(3, False)

            @pl.when(is_early & (half == 1) & (i == 3 - x))
            def _():
                send_help()
            return 0
        lax.fori_loop(0, 4, one, 0)
        return 0

    lax.fori_loop(0, 2, both, 0)

    @pl.when(is_early)
    def _():
        o_ref[...] = (acc[0] / l[0]).astype(jnp.bfloat16)

    @pl.when(is_late)
    def _():
        query_copy.wait_send()
        log_copy.wait_recv()
        out_copy.wait_recv()
        for i in range(rows // 128):
            at = slice(i * 128, (i + 1) * 128)
            log = jnp.sum(jnp.where(eye, lh[i:i + 1], 0.0), axis=1, keepdims=True)
            mine = m[0, at]
            top = jnp.maximum(mine, log)
            w_mine, w_help = jnp.exp2(mine - top), jnp.exp2(log - top)
            total = l[0, at] * w_mine + w_help
            mixed = acc[0, at] * w_mine + qh[at].astype(jnp.float32) * w_help
            o_ref[at] = (mixed / total).astype(jnp.bfloat16)

    @pl.when(z == 0)
    def _():
        log_copy.wait_send()
        out_copy.wait_send()
    for d in range(1, 8):
        scatter(d).wait_send()
    for r in range(4):
        kinds = [XP, XM, SIB, SIB_XP, SIB_XM, SIB_X2] + ([X2, Y_X2] if r % 2 == 0 else []) + ([Y] if r else [])
        for kind in kinds:
            piece(kind, r, c, to_sib).wait_send()
        for kind, when in ((UP, z == 0), (SIB_UP, z == 1)):
            @pl.when(when)
            def _(kind=kind):
                piece(kind, r, c, to_sib).wait_send()


def per_device(queries, key_states, value_states):
    rows, _, width = queries.shape
    f32, bf16 = jnp.float32, jnp.bfloat16
    dma = pltpu.SemaphoreType.DMA
    out = pl.pallas_call(
        kernel,
        out_shape=jax.ShapeDtypeStruct((rows, width), bf16),
        in_specs=[pl.BlockSpec(memory_space=pltpu.HBM)] * 3,
        out_specs=pl.BlockSpec(memory_space=pltpu.VMEM),
        scratch_shapes=[
            pltpu.VMEM((rows, width), bf16),
            pltpu.VMEM(key_states.shape, bf16),
            pltpu.VMEM(value_states.shape, bf16),
            pltpu.VMEM((BLOCKS, 4, 8, 64, width), bf16),
            pltpu.VMEM((8, 64, width), bf16),
            pltpu.VMEM((256, width), f32),
            pltpu.VMEM((2, rows, 2 * width), bf16),
            pltpu.VMEM((rows, width), bf16),
            pltpu.VMEM((rows, width), bf16),
            pltpu.VMEM((8, 128), f32),
            pltpu.VMEM((8, 128), f32),
            pltpu.VMEM((2, rows, width), f32),
            pltpu.VMEM((2, rows, width), f32),
            pltpu.VMEM((2, rows, width), f32),
            dma((11, 4)),
            dma((BLOCKS, 4)),
            dma((8,)),
            dma((8,)),
            dma((2,)),
            dma((2,)),
            dma((2,)),
            dma((3,)),
        ],
        name="folded_attention",
        cost_estimate=pl.CostEstimate(flops=4 * 128 * 8 * 1024 * 1024, bytes_accessed=2**20, transcendentals=2**23),
        compiler_params=pltpu.CompilerParams(
            collective_id=0, has_side_effects=True, vmem_limit_bytes=62 * 2**20),
    )(queries.reshape(rows, width), key_states, value_states)
    return out[:, None, :]


def solution(mesh):
    return jax.shard_map(
        per_device,
        mesh=mesh,
        in_specs=(
            P("ctx", "head", None),
            P(("ctx", "head"), None, None),
            P(("ctx", "head"), None, None),
        ),
        out_specs=P("ctx", "head", None),
        check_vma=False,
    )
```

```python
import functools
import math

import jax
import jax.numpy as jnp
from jax import lax
from jax.experimental import pallas as pl
from jax.experimental.pallas import tpu as pltpu
from jax.sharding import PartitionSpec as P

MESH = pl.DeviceIdType.MESH
NEG = -1e30
BLOCKS = 16
QT = 256
XP, XM, X2, SIB, UP, SIB_XP, SIB_XM, SIB_X2, Y_X2, SIB_UP, Y = range(11)


def kernel(q_hbm, k_hbm, v_hbm, o_ref, q_ref, k_ref, v_ref, kv, stage, wide, qc, qh, oh, lh_out,
           help_o, help_l, m, l, acc, ss, rs, p1s, p1r, qsem, ssem, osem, isem):
    c = lax.axis_index("ctx")
    h = lax.axis_index("head")
    z, x, core = c // 8, (c // 2) % 4, c % 2
    group, lane = h // 4, h % 4
    rows = q_ref.shape[0]
    tiles = rows // QT

    def quarter(r):
        return (lane + r // 2) % 2 + 2 * ((lane // 2 + r % 2) % 2)

    def device(x_, z_, core_, lane_):
        return {"ctx": z_ * 8 + x_ * 2 + core_, "head": group * 4 + lane_}

    xp, xm, x2 = (x + 1) % 4, (x + 3) % 4, (x + 2) % 4
    to_xp, to_xm, to_x2 = (device(t, z, core, lane) for t in (xp, xm, x2))
    to_sib = device(x, z, 1 - core, lane)
    to_z = device(x, 1 - z, core, lane)
    to_mirror = device(3 - x, 1 - z, 1 - core, lane)
    to_y = device(x, z, core, quarter(2))
    to_group = [{"ctx": c, "head": ((group + d % 8) % 8) * 4 + quarter(d // 8)} for d in range(16)]

    barrier = pltpu.get_barrier_semaphore()
    partners = to_group[1:] + [to_y, to_xp, to_xm, to_x2, to_sib, to_z, to_mirror]
    for partner in partners:
        pl.semaphore_signal(barrier, inc=1, device_id=partner, device_id_type=MESH)

    loads = [pltpu.make_async_copy(src, dst, isem.at[i])
             for i, (src, dst) in enumerate(((k_hbm, k_ref), (v_hbm, v_ref), (q_hbm, q_ref)))]
    for copy in loads:
        copy.start()
    loads[0].wait()
    loads[1].wait()

    for ref, first in ((k_ref, 0), (v_ref, 32)):
        wide[...] = ref[...].astype(jnp.float32).reshape(wide.shape)
        for g in range(8):
            stage[g, first:first + 32] = wide[pl.ds(g, 32, stride=8), :].astype(jnp.bfloat16)
    kv[c, lane, group] = stage[group]

    scale = math.log2(math.e) / math.sqrt(q_ref.shape[1])

    def split_scaled(job, src):
        def one(i, _):
            r = pl.ds(pl.multiple_of(i * QT, QT), QT)
            scaled = src[r].astype(jnp.float32) * scale
            high = scaled.astype(jnp.bfloat16)
            qc[job, r, :128] = high
            qc[job, r, 128:] = (scaled - high.astype(jnp.float32)).astype(jnp.bfloat16)
            return 0
        lax.fori_loop(0, tiles, one, 0)

    loads[2].wait()
    split_scaled(0, q_ref)
    m[...] = jnp.full(m.shape, NEG, jnp.float32)
    l[...] = jnp.zeros(l.shape, jnp.float32)
    acc[...] = jnp.zeros(acc.shape, jnp.float32)

    pl.semaphore_wait(barrier, len(partners))

    def remote(src, dst, send, recv, to):
        return pltpu.make_async_remote_copy(
            src_ref=src, dst_ref=dst, send_sem=send, recv_sem=recv, device_id=to, device_id_type=MESH)

    def scatter(d):
        return remote(stage.at[(group + d % 8) % 8], kv.at[c, lane, group], p1s.at[d], p1r.at[d], to_group[d])

    for d in (4, 3, 5, 2, 6, 1, 7, 12, 11, 13, 10, 14, 9, 15, 8):
        scatter(d).start()
    query_copy = remote(q_ref, qh, qsem.at[0], qsem.at[1], to_mirror)
    is_late = z == 1
    is_early = z == 0

    pl.when(is_late & (x > 0))(query_copy.start)

    def piece(kind, r, block, to):
        q = quarter(r)
        return remote(kv.at[block, q], kv.at[block, q], ss.at[kind, r], rs.at[block, q], to)

    def landed(r, block):
        piece(0, r, block, to_sib).wait_recv()

    def from_chip(x_):
        return 2 * x_ + 8 * z * (x_ < x).astype(jnp.int32)

    own_up = 2 * x + core
    own_goes = {XP: x < 3, XM: x < 2 - z, X2: x < 3 - z}
    up_goes = {XP: is_late & (x == 3), XM: is_late & (x > 0), X2: is_late & (x > 1)}
    has_xp = is_late | (x == 0) | (x == 3)
    has_xm = is_late | (x > 0)
    has_x2 = is_late | (x != 1)
    helps = is_early & (x < 3)
    helped = is_late & (x > 0)
    targets = {XP: to_xp, XM: to_xm, X2: to_x2}

    def kinds_x(direct):
        return (X2, XP, XM) if direct else (XP, XM)

    def own_quarter(r, direct, first=False):
        if not first:
            landed(r, c)
        @pl.when(z == 0)
        def _():
            piece(UP, r, c, to_z).start()

        for kind in kinds_x(direct):
            @pl.when(own_goes[kind])
            def _(kind=kind):
                piece(kind, r, c, targets[kind]).start()

        piece(SIB, r, c, to_sib).start()

    def up_quarter(r, direct):
        @pl.when(is_late)
        def _():
            landed(r, own_up)
            for kind in kinds_x(direct):
                @pl.when(up_goes[kind])
                def _(kind=kind):
                    piece(kind, r, own_up, targets[kind]).start()
            piece(SIB_UP, r, own_up, to_sib).start()

    def x_quarters(r):
        def take(kind, source):
            landed(r, from_chip(source) + core)
            piece(kind, r, from_chip(source) + core, to_sib).start()

        pl.when(has_xp)(lambda: take(SIB_XP, xp))
        pl.when(has_xm)(lambda: take(SIB_XM, xm))

    def x2_quarter(r, direct):
        @pl.when(has_x2)
        def _():
            block = from_chip(x2) + core
            landed(r, block)
            if direct:
                piece(Y_X2, r, block, to_y).start()
            piece(SIB_X2, r, block, to_sib).start()

    def sib_own(r):
        landed(r, c + 1 - 2 * core)

    def sib_up(r):
        landed(r, own_up + 1 - 2 * core)

    def sib_x(r):
        @pl.when(has_xp)
        def _():
            landed(r, from_chip(xp) + 1 - core)

        @pl.when(has_xm)
        def _():
            landed(r, from_chip(xm) + 1 - core)

    def sib_x2(r):
        @pl.when(has_x2)
        def _():
            landed(r, from_chip(x2) + 1 - core)

    def attend(job, parts):
        scores = []
        for tile, (keys, values, mask) in enumerate(parts):
            at = slice(tile * QT, (tile + 1) * QT)
            score = lax.dot_general(qc[job, at], jnp.concatenate([keys, keys], axis=1),
                                    (((1,), (1,)), ((), ())), preferred_element_type=jnp.float32)
            scores.append(score if mask is None else jnp.where(mask, score, NEG))
        rounded, shrinks = [], []
        for tile, score in enumerate(scores):
            at = slice(tile * QT, (tile + 1) * QT)
            before = m[job, at]
            now = jnp.maximum(before, jnp.max(score, axis=1, keepdims=True))
            m[job, at] = now
            shrinks.append(jnp.exp2(before - now))
            across = jnp.concatenate([now] * (score.shape[1] // 128), axis=1)
            rounded.append(jnp.exp2(score - across).astype(jnp.bfloat16))
        for tile, (_, values, _) in enumerate(parts):
            at = slice(tile * QT, (tile + 1) * QT)
            mixed = jnp.dot(rounded[tile], jnp.concatenate([values, jnp.ones_like(values)], axis=1),
                            preferred_element_type=jnp.float32)
            acc[job, at] = acc[job, at] * shrinks[tile] + mixed[:, :128]
            l[job, at] = l[job, at] * shrinks[tile] + mixed[:, 128:]

    def load(blocks, half, first, count):
        parts = [(b, quarter(2 * half + i)) for b in blocks for i in range(2)]
        def side(at):
            return jnp.concatenate(
                [kv[b, q, pl.ds(first, count), at:at + 32, :].reshape(count * 32, 128) for b, q in parts], axis=0)
        return side(0), side(32)

    def diagonal(half):
        parts = []
        for tile in range(tiles):
            count = 2 * (tile + 1)
            keys, values = load([c], half, 0, count)
            spot = lax.broadcasted_iota(jnp.int32, (1, count * 64), 1)
            which = jnp.where(spot < count * 32, quarter(2 * half), quarter(2 * half + 1))
            inner = spot % (count * 32)
            key_pos = (inner // 32) * 128 + which * 32 + inner % 32
            query_pos = tile * QT + lax.broadcasted_iota(jnp.int32, (QT, 1), 0)
            parts.append((keys, values, key_pos <= query_pos))
        attend(0, parts)

    def single(half):
        keys, values = load([2 * x], half, 0, 8)
        attend(0, [(keys, values, None)] * tiles)

    def by_x(a0, a1, a2, a3):
        return jnp.where(x == 0, a0, jnp.where(x == 1, a1, jnp.where(x == 2, a2, a3)))

    def by_step(i, a0, a1, a2):
        return jnp.where(i == 0, a0, jnp.where(i == 1, a1, a2))

    def pair(i, half):
        late_base = from_chip(by_step(i - 1, xp, xm, x2))
        late_a = jnp.where(i == 0, own_up, late_base)
        late_b = jnp.where(i == 0, 2 * x + jnp.where(core == 0, 1, 8), late_base + 1)
        chip_a = by_step(i - 1, by_x(0, 1, 1, 0), by_x(1, 0, 0, 2), by_x(2, 0, 0, 1))
        job_a = by_step(i - 1, by_x(1, 1, 0, 0), by_x(1, 0, 0, 0), by_x(1, 1, 1, 0))
        chip_b = by_step(i - 1, by_x(0, 1, 0, 0), by_x(1, 0, 1, 2), by_x(2, 0, 0, 1))
        job_b = by_step(i - 1, by_x(1, 1, 1, 0), by_x(1, 1, 0, 0), by_x(1, 0, 0, 0))
        early_a = 2 * jnp.where(half == 0, chip_a, chip_b)
        job = jnp.where(is_late, 0, jnp.where(half == 0, job_a, job_b))
        blocks = [jnp.where(is_late, late_a, early_a), jnp.where(is_late, late_b, early_a + 1)]
        keys, values = load(blocks, half, 0, 8)
        attend(job, [(keys, values, None)] * tiles)

    def exchange(r):
        q = quarter(r)
        return remote(kv.at[c, q], kv.at[c, q], ss.at[Y, r], rs.at[c, q], to_y)

    for r, pieces in ((0, range(1, 8)), (1, range(8, 16))):
        for d in pieces:
            scatter(d).wait_recv()
        exchange(r).start()
        own_quarter(r, True, True)

    eye = (lax.broadcasted_iota(jnp.int32, (128, 128), 0) == lax.broadcasted_iota(jnp.int32, (128, 128), 1))
    log_copy = remote(lh_out, help_l, ssem.at[0], ssem.at[1], to_mirror)
    part_copies = [remote(oh.at[pl.ds(i * QT, QT)], help_o.at[pl.ds(i * QT, QT)], osem.at[i], osem.at[tiles + i], to_mirror)
                   for i in range(tiles)]

    def send_part():
        for i in range(rows // 128):
            at = slice(i * 128, (i + 1) * 128)
            log = m[1, at] + jnp.log2(l[1, at])
            lh_out[i:i + 1] = jnp.sum(jnp.where(eye, log, 0.0), axis=0, keepdims=True)
        log_copy.start()
        for i, copy in enumerate(part_copies):
            at = slice(i * QT, (i + 1) * QT)
            oh[at] = (acc[1, at] / l[1, at]).astype(jnp.bfloat16)
            copy.start()

    def both(half, _):
        first = half == 0
        r0, r1 = 2 * half, 2 * half + 1

        def one(i, _):
            @pl.when(jnp.where(is_early & (half == 1), i == 4, i == 0))
            def _():
                diagonal(half)

            @pl.when(first & (i == 0))
            def _():
                own_quarter(2, False)
                up_quarter(0, True)
                pl.when(is_early)(lambda: x_quarters(0))
                own_quarter(3, False)
                up_quarter(1, True)
                pl.when(is_early)(lambda: x2_quarter(0, True))

                @pl.when(helps)
                def _():
                    query_copy.wait_recv()
                    split_scaled(1, qh)

            @pl.when(i == 0)
            def _():
                sib_own(r0)
                sib_own(r1)

                @pl.when(is_late)
                def _():
                    sib_up(r0)
                    sib_up(r1)

            @pl.when(first & (i == 1))
            def _():
                up_quarter(2, False)

                @pl.when(is_late)
                def _():
                    x_quarters(0)
                    x2_quarter(0, True)
                x_quarters(1)
                up_quarter(3, False)
                x2_quarter(1, True)

            @pl.when(i == 1)
            def _():
                sib_x(r0)
                sib_x(r1)

            @pl.when(first & (i == 2))
            def _():
                x_quarters(2)

            @pl.when(i == jnp.where(is_late, 3, jnp.where(first, 2, 1)))
            def _():
                sib_x2(r0)
                sib_x2(r1)

            @pl.when(first & (i == 3))
            def _():
                x2_quarter(2, False)
                x_quarters(3)

            @pl.when((core == 1) & (i == 0))
            def _():
                single(half)

            @pl.when((i < 4) & (is_late | (i > 0)))
            def _():
                pair(i, half)

            @pl.when(helps & (half == 1) & (i == 3 - x))
            def _():
                send_part()
            return 0
        lax.fori_loop(0, 5, one, 0)
        pl.when(first)(lambda: x2_quarter(3, False))
        return 0

    lax.fori_loop(0, 2, both, 0)

    @pl.when(jnp.logical_not(helped))
    def _():
        o_ref[...] = (acc[0] / l[0]).astype(jnp.bfloat16)

    @pl.when(helped)
    def _():
        log_copy.wait_recv()
        for i in range(rows // 128):
            if i % (QT // 128) == 0:
                part_copies[i * 128 // QT].wait_recv()
            at = slice(i * 128, (i + 1) * 128)
            log = jnp.sum(jnp.where(eye, help_l[i:i + 1], 0.0), axis=1, keepdims=True)
            mine = m[0, at]
            top = jnp.maximum(mine, log)
            w_mine, w_help = jnp.exp2(mine - top), jnp.exp2(log - top)
            total = l[0, at] * w_mine + w_help
            mixed = acc[0, at] * w_mine + help_o[at].astype(jnp.float32) * w_help
            o_ref[at] = (mixed / total).astype(jnp.bfloat16)
        query_copy.wait_send()

    @pl.when(helps)
    def _():
        for copy in [log_copy] + part_copies:
            copy.wait_send()
    for d in range(1, 16):
        scatter(d).wait_send()
    for r in range(4):
        sent = [(XP, own_goes[XP] | up_goes[XP]), (XM, own_goes[XM] | up_goes[XM]), (SIB, None), (SIB_XP, has_xp),
                (SIB_XM, has_xm), (SIB_X2, has_x2), (UP, is_early), (SIB_UP, is_late)]
        if r < 2:
            sent += [(X2, own_goes[X2] | up_goes[X2]), (Y_X2, has_x2), (Y, None)]
        for kind, when in sent:
            wait = piece(kind, r, c, to_sib).wait_send
            if when is None:
                wait()
            else:
                pl.when(when)(wait)


def per_device(queries, key_states, value_states):
    rows, _, width = queries.shape
    f32, bf16 = jnp.float32, jnp.bfloat16
    dma = pltpu.SemaphoreType.DMA
    out = pl.pallas_call(
        kernel,
        out_shape=jax.ShapeDtypeStruct((rows, width), bf16),
        in_specs=[pl.BlockSpec(memory_space=pltpu.HBM)] * 3,
        out_specs=pl.BlockSpec(memory_space=pltpu.VMEM),
        scratch_shapes=[
            pltpu.VMEM((rows, width), bf16),
            pltpu.VMEM(key_states.shape, bf16),
            pltpu.VMEM(value_states.shape, bf16),
            pltpu.VMEM((BLOCKS, 4, 8, 64, width), bf16),
            pltpu.VMEM((8, 64, width), bf16),
            pltpu.VMEM((256, width), f32),
            pltpu.VMEM((2, rows, 2 * width), bf16),
            pltpu.VMEM((rows, width), bf16),
            pltpu.VMEM((rows, width), bf16),
            pltpu.VMEM((8, 128), f32),
            pltpu.VMEM((rows, width), bf16),
            pltpu.VMEM((8, 128), f32),
            pltpu.VMEM((2, rows, width), f32),
            pltpu.VMEM((2, rows, width), f32),
            pltpu.VMEM((2, rows, width), f32),
            dma((11, 4)),
            dma((BLOCKS, 4)),
            dma((16,)),
            dma((16,)),
            dma((2,)),
            dma((2,)),
            dma((8,)),
            dma((3,)),
        ],
        name="folded_attention",
        cost_estimate=pl.CostEstimate(flops=4 * 128 * 8 * 1024 * 1024, bytes_accessed=2**20, transcendentals=2**23),
        compiler_params=pltpu.CompilerParams(
            collective_id=0, has_side_effects=True, vmem_limit_bytes=62 * 2**20),
    )(queries.reshape(rows, width), key_states, value_states)
    return out[:, None, :]


def solution(mesh):
    return jax.shard_map(
        per_device,
        mesh=mesh,
        in_specs=(
            P("ctx", "head", None),
            P(("ctx", "head"), None, None),
            P(("ctx", "head"), None, None),
        ),
        out_specs=P("ctx", "head", None),
        check_vma=False,
    )
```

```python
import functools
import math

import jax
import jax.numpy as jnp
from jax import lax
from jax.experimental import pallas as pl
from jax.experimental.pallas import tpu as pltpu
from jax.sharding import PartitionSpec as P

MESH = pl.DeviceIdType.MESH
NEG = -1e30
BLOCKS = 16
QT = 256
XP, XM, X2, SIB, UP, SIB_XP, SIB_XM, SIB_X2, Y_X2, SIB_UP, Y = range(11)


def kernel(q_hbm, k_hbm, v_hbm, o_ref, q_ref, k_ref, v_ref, kv, stage, wide, qc, qh, oh, lh_out,
           help_o, help_l, m, l, acc, ss, rs, p1s, p1r, qsem, ssem, osem, isem):
    c = lax.axis_index("ctx")
    h = lax.axis_index("head")
    z, x, core = c // 8, (c // 2) % 4, c % 2
    group, lane = h // 4, h % 4
    rows = q_ref.shape[0]
    tiles = rows // QT

    def quarter(r):
        return (lane + r // 2) % 2 + 2 * ((lane // 2 + r % 2) % 2)

    def device(x_, z_, core_, lane_):
        return {"ctx": z_ * 8 + x_ * 2 + core_, "head": group * 4 + lane_}

    xp, xm, x2 = (x + 1) % 4, (x + 3) % 4, (x + 2) % 4
    to_xp, to_xm, to_x2 = (device(t, z, core, lane) for t in (xp, xm, x2))
    to_sib = device(x, z, 1 - core, lane)
    to_z = device(x, 1 - z, core, lane)
    to_mirror = device(3 - x, 1 - z, 1 - core, lane)
    to_y = device(x, z, core, quarter(2))
    to_group = [{"ctx": c, "head": ((group + d % 8) % 8) * 4 + quarter(d // 8)} for d in range(16)]

    barrier = pltpu.get_barrier_semaphore()
    partners = to_group[1:] + [to_y, to_xp, to_xm, to_x2, to_sib, to_z, to_mirror]
    for partner in partners:
        pl.semaphore_signal(barrier, inc=1, device_id=partner, device_id_type=MESH)

    loads = [pltpu.make_async_copy(src, dst, isem.at[i])
             for i, (src, dst) in enumerate(((k_hbm, k_ref), (v_hbm, v_ref), (q_hbm, q_ref)))]
    for copy in loads:
        copy.start()
    loads[0].wait()
    loads[1].wait()

    for ref, first in ((k_ref, 0), (v_ref, 32)):
        wide[...] = ref[...].astype(jnp.float32).reshape(wide.shape)
        for g in range(8):
            stage[g, first:first + 32] = wide[pl.ds(g, 32, stride=8), :].astype(jnp.bfloat16)
    kv[c, lane, group] = stage[group]

    scale = math.log2(math.e) / math.sqrt(q_ref.shape[1])

    def split_scaled(job, src):
        def one(i, _):
            r = pl.ds(pl.multiple_of(i * QT, QT), QT)
            scaled = src[r].astype(jnp.float32) * scale
            high = scaled.astype(jnp.bfloat16)
            qc[job, r, :128] = high
            qc[job, r, 128:] = (scaled - high.astype(jnp.float32)).astype(jnp.bfloat16)
            return 0
        lax.fori_loop(0, tiles, one, 0)

    loads[2].wait()
    split_scaled(0, q_ref)
    m[...] = jnp.full(m.shape, NEG, jnp.float32)
    l[...] = jnp.zeros(l.shape, jnp.float32)
    acc[...] = jnp.zeros(acc.shape, jnp.float32)

    pl.semaphore_wait(barrier, len(partners))

    def remote(src, dst, send, recv, to):
        return pltpu.make_async_remote_copy(
            src_ref=src, dst_ref=dst, send_sem=send, recv_sem=recv, device_id=to, device_id_type=MESH)

    def scatter(d):
        return remote(stage.at[(group + d % 8) % 8], kv.at[c, lane, group], p1s.at[d], p1r.at[d], to_group[d])

    for d in (4, 3, 5, 2, 6, 1, 7, 12, 11, 13, 10, 14, 9, 15, 8):
        scatter(d).start()
    query_copy = remote(q_ref, qh, qsem.at[0], qsem.at[1], to_mirror)
    is_late = z == 1
    is_early = z == 0

    pl.when(is_late & (x > 0))(query_copy.start)

    def piece(kind, r, block, to):
        q = quarter(r)
        return remote(kv.at[block, q], kv.at[block, q], ss.at[kind, r], rs.at[block, q], to)

    def landed(r, block):
        piece(0, r, block, to_sib).wait_recv()

    def from_chip(x_):
        return 2 * x_ + 8 * z * (x_ < x).astype(jnp.int32)

    own_up = 2 * x + core
    own_goes = {XP: x < 3, XM: x < 2 - z, X2: x < 3 - z}
    up_goes = {XP: is_late & (x == 3), XM: is_late & (x > 0), X2: is_late & (x > 1)}
    has_xp = is_late | (x == 0) | (x == 3)
    has_xm = is_late | (x > 0)
    has_x2 = is_late | (x != 1)
    helps = is_early & (x < 3)
    helped = is_late & (x > 0)
    targets = {XP: to_xp, XM: to_xm, X2: to_x2}

    def kinds_x(direct):
        return (X2, XP, XM) if direct else (XP, XM)

    def own_quarter(r, direct, first=False):
        if not first:
            landed(r, c)
        @pl.when(z == 0)
        def _():
            piece(UP, r, c, to_z).start()

        for kind in kinds_x(direct):
            @pl.when(own_goes[kind])
            def _(kind=kind):
                piece(kind, r, c, targets[kind]).start()

        piece(SIB, r, c, to_sib).start()

    def up_quarter(r, direct):
        @pl.when(is_late)
        def _():
            landed(r, own_up)
            for kind in kinds_x(direct):
                @pl.when(up_goes[kind])
                def _(kind=kind):
                    piece(kind, r, own_up, targets[kind]).start()
            piece(SIB_UP, r, own_up, to_sib).start()

    def x_quarters(r):
        def take(kind, source):
            landed(r, from_chip(source) + core)
            piece(kind, r, from_chip(source) + core, to_sib).start()

        pl.when(has_xp)(lambda: take(SIB_XP, xp))
        pl.when(has_xm)(lambda: take(SIB_XM, xm))

    def x2_quarter(r, direct):
        @pl.when(has_x2)
        def _():
            block = from_chip(x2) + core
            landed(r, block)
            if direct:
                piece(Y_X2, r, block, to_y).start()
            piece(SIB_X2, r, block, to_sib).start()

    def sib_own(r):
        landed(r, c + 1 - 2 * core)

    def sib_up(r):
        landed(r, own_up + 1 - 2 * core)

    def sib_x(r):
        @pl.when(has_xp)
        def _():
            landed(r, from_chip(xp) + 1 - core)

        @pl.when(has_xm)
        def _():
            landed(r, from_chip(xm) + 1 - core)

    def sib_x2(r):
        @pl.when(has_x2)
        def _():
            landed(r, from_chip(x2) + 1 - core)

    def attend(job, parts):
        scores = []
        for tile, (keys, values, mask) in enumerate(parts):
            at = slice(tile * QT, (tile + 1) * QT)
            score = lax.dot_general(qc[job, at], jnp.concatenate([keys, keys], axis=1),
                                    (((1,), (1,)), ((), ())), preferred_element_type=jnp.float32)
            scores.append(score if mask is None else jnp.where(mask, score, NEG))
        rounded, shrinks = [], []
        for tile, score in enumerate(scores):
            at = slice(tile * QT, (tile + 1) * QT)
            before = m[job, at]
            now = jnp.maximum(before, jnp.max(score, axis=1, keepdims=True))
            m[job, at] = now
            shrinks.append(jnp.exp2(before - now))
            across = jnp.concatenate([now] * (score.shape[1] // 128), axis=1)
            rounded.append(jnp.exp2(score - across).astype(jnp.bfloat16))
        for tile, (_, values, _) in enumerate(parts):
            at = slice(tile * QT, (tile + 1) * QT)
            mixed = jnp.dot(rounded[tile], jnp.concatenate([values, jnp.ones_like(values)], axis=1),
                            preferred_element_type=jnp.float32)
            acc[job, at] = acc[job, at] * shrinks[tile] + mixed[:, :128]
            l[job, at] = l[job, at] * shrinks[tile] + mixed[:, 128:]

    def load(blocks, half, first, count):
        parts = [(b, quarter(2 * half + i)) for b in blocks for i in range(2)]
        def side(at):
            return jnp.concatenate(
                [kv[b, q, pl.ds(first, count), at:at + 32, :].reshape(count * 32, 128) for b, q in parts], axis=0)
        return side(0), side(32)

    def diagonal(half):
        parts = []
        for tile in range(tiles):
            count = 2 * (tile + 1)
            keys, values = load([c], half, 0, count)
            spot = lax.broadcasted_iota(jnp.int32, (1, count * 64), 1)
            which = jnp.where(spot < count * 32, quarter(2 * half), quarter(2 * half + 1))
            inner = spot % (count * 32)
            key_pos = (inner // 32) * 128 + which * 32 + inner % 32
            query_pos = tile * QT + lax.broadcasted_iota(jnp.int32, (QT, 1), 0)
            parts.append((keys, values, key_pos <= query_pos))
        attend(0, parts)

    def single(half):
        keys, values = load([2 * x], half, 0, 8)
        attend(0, [(keys, values, None)] * tiles)

    def by_x(a0, a1, a2, a3):
        return jnp.where(x == 0, a0, jnp.where(x == 1, a1, jnp.where(x == 2, a2, a3)))

    def by_step(i, a0, a1, a2):
        return jnp.where(i == 0, a0, jnp.where(i == 1, a1, a2))

    def pair(i, half):
        late_base = from_chip(by_step(i - 1, xp, xm, x2))
        late_a = jnp.where(i == 0, own_up, late_base)
        late_b = jnp.where(i == 0, 2 * x + jnp.where(core == 0, 1, 8), late_base + 1)
        chip_a = by_step(i - 1, by_x(0, 1, 1, 0), by_x(1, 0, 0, 2), by_x(2, 0, 0, 1))
        job_a = by_step(i - 1, by_x(1, 1, 0, 0), by_x(1, 0, 0, 0), by_x(1, 1, 1, 0))
        chip_b = by_step(i - 1, by_x(0, 1, 0, 0), by_x(1, 0, 1, 2), by_x(2, 0, 0, 1))
        job_b = by_step(i - 1, by_x(1, 1, 1, 0), by_x(1, 1, 0, 0), by_x(1, 0, 0, 0))
        early_a = 2 * jnp.where(half == 0, chip_a, chip_b)
        job = jnp.where(is_late, 0, jnp.where(half == 0, job_a, job_b))
        blocks = [jnp.where(is_late, late_a, early_a), jnp.where(is_late, late_b, early_a + 1)]
        keys, values = load(blocks, half, 0, 8)
        attend(job, [(keys, values, None)] * tiles)

    def exchange(r):
        q = quarter(r)
        return remote(kv.at[c, q], kv.at[c, q], ss.at[Y, r], rs.at[c, q], to_y)

    for r, pieces in ((0, range(1, 8)), (1, range(8, 16))):
        for d in pieces:
            scatter(d).wait_recv()
        exchange(r).start()
        own_quarter(r, True, True)

    eye = (lax.broadcasted_iota(jnp.int32, (128, 128), 0) == lax.broadcasted_iota(jnp.int32, (128, 128), 1))
    log_copy = remote(lh_out, help_l, ssem.at[0], ssem.at[1], to_mirror)
    part_copies = [remote(oh.at[pl.ds(i * QT, QT)], help_o.at[pl.ds(i * QT, QT)], osem.at[i], osem.at[tiles + i], to_mirror)
                   for i in range(tiles)]

    def send_part():
        for i in range(rows // 128):
            at = slice(i * 128, (i + 1) * 128)
            log = m[1, at] + jnp.log2(l[1, at])
            lh_out[i:i + 1] = jnp.sum(jnp.where(eye, log, 0.0), axis=0, keepdims=True)
        log_copy.start()
        for i, copy in enumerate(part_copies):
            at = slice(i * QT, (i + 1) * QT)
            oh[at] = (acc[1, at] / l[1, at]).astype(jnp.bfloat16)
            copy.start()

    def both(half, _):
        first = half == 0
        r0, r1 = 2 * half, 2 * half + 1

        def one(i, _):
            @pl.when(jnp.where(is_early & (half == 1), i == 4, i == 0))
            def _():
                diagonal(half)

            @pl.when(first & (i == 0))
            def _():
                own_quarter(2, False)
                up_quarter(0, True)
                pl.when(is_early)(lambda: x_quarters(0))
                own_quarter(3, False)
                up_quarter(1, True)
                pl.when(is_early)(lambda: x2_quarter(0, True))

                @pl.when(helps)
                def _():
                    query_copy.wait_recv()
                    split_scaled(1, qh)

            @pl.when((half == 1) & (i == 0))
            def _():
                x2_quarter(2, False)
                x_quarters(3)
                x2_quarter(3, False)

            @pl.when(i == 0)
            def _():
                sib_own(r0)
                sib_own(r1)

                @pl.when(is_late)
                def _():
                    sib_up(r0)
                    sib_up(r1)

            @pl.when(first & (i == 1))
            def _():
                up_quarter(2, False)

                @pl.when(is_late)
                def _():
                    x_quarters(0)
                    x2_quarter(0, True)
                x_quarters(1)
                up_quarter(3, False)
                x2_quarter(1, True)

            @pl.when(i == jnp.where(is_early & (x < 2), 2, 1))
            def _():
                sib_x(r0)
                sib_x(r1)

            @pl.when(first & (i == 2))
            def _():
                x_quarters(2)

            @pl.when(i == jnp.where(is_late | (x != 2), 3, jnp.where(first, 2, 1)))
            def _():
                sib_x2(r0)
                sib_x2(r1)

            @pl.when((core == 1) & (i == jnp.where(is_early & (half == 1), 4, 0)))
            def _():
                single(half)

            @pl.when((i < 4) & (is_late | (i > 0)))
            def _():
                pair(i, half)

            @pl.when(helps & (half == 1) & (i == 3 - x))
            def _():
                send_part()
            return 0
        lax.fori_loop(0, 5, one, 0)
        return 0

    lax.fori_loop(0, 2, both, 0)

    @pl.when(jnp.logical_not(helped))
    def _():
        o_ref[...] = (acc[0] / l[0]).astype(jnp.bfloat16)

    @pl.when(helped)
    def _():
        log_copy.wait_recv()
        for i in range(rows // 128):
            if i % (QT // 128) == 0:
                part_copies[i * 128 // QT].wait_recv()
            at = slice(i * 128, (i + 1) * 128)
            log = jnp.sum(jnp.where(eye, help_l[i:i + 1], 0.0), axis=1, keepdims=True)
            mine = m[0, at]
            top = jnp.maximum(mine, log)
            w_mine, w_help = jnp.exp2(mine - top), jnp.exp2(log - top)
            total = l[0, at] * w_mine + w_help
            mixed = acc[0, at] * w_mine + help_o[at].astype(jnp.float32) * w_help
            o_ref[at] = (mixed / total).astype(jnp.bfloat16)
        query_copy.wait_send()

    @pl.when(helps)
    def _():
        for copy in [log_copy] + part_copies:
            copy.wait_send()
    for d in range(1, 16):
        scatter(d).wait_send()
    for r in range(4):
        sent = [(XP, own_goes[XP] | up_goes[XP]), (XM, own_goes[XM] | up_goes[XM]), (SIB, None), (SIB_XP, has_xp),
                (SIB_XM, has_xm), (SIB_X2, has_x2), (UP, is_early), (SIB_UP, is_late)]
        if r < 2:
            sent += [(X2, own_goes[X2] | up_goes[X2]), (Y_X2, has_x2), (Y, None)]
        for kind, when in sent:
            wait = piece(kind, r, c, to_sib).wait_send
            if when is None:
                wait()
            else:
                pl.when(when)(wait)


def per_device(queries, key_states, value_states):
    rows, _, width = queries.shape
    f32, bf16 = jnp.float32, jnp.bfloat16
    dma = pltpu.SemaphoreType.DMA
    out = pl.pallas_call(
        kernel,
        out_shape=jax.ShapeDtypeStruct((rows, width), bf16),
        in_specs=[pl.BlockSpec(memory_space=pltpu.HBM)] * 3,
        out_specs=pl.BlockSpec(memory_space=pltpu.VMEM),
        scratch_shapes=[
            pltpu.VMEM((rows, width), bf16),
            pltpu.VMEM(key_states.shape, bf16),
            pltpu.VMEM(value_states.shape, bf16),
            pltpu.VMEM((BLOCKS, 4, 8, 64, width), bf16),
            pltpu.VMEM((8, 64, width), bf16),
            pltpu.VMEM((256, width), f32),
            pltpu.VMEM((2, rows, 2 * width), bf16),
            pltpu.VMEM((rows, width), bf16),
            pltpu.VMEM((rows, width), bf16),
            pltpu.VMEM((8, 128), f32),
            pltpu.VMEM((rows, width), bf16),
            pltpu.VMEM((8, 128), f32),
            pltpu.VMEM((2, rows, width), f32),
            pltpu.VMEM((2, rows, width), f32),
            pltpu.VMEM((2, rows, width), f32),
            dma((11, 4)),
            dma((BLOCKS, 4)),
            dma((16,)),
            dma((16,)),
            dma((2,)),
            dma((2,)),
            dma((8,)),
            dma((3,)),
        ],
        name="folded_attention",
        cost_estimate=pl.CostEstimate(flops=4 * 128 * 8 * 1024 * 1024, bytes_accessed=2**20, transcendentals=2**23),
        compiler_params=pltpu.CompilerParams(
            collective_id=0, has_side_effects=True, vmem_limit_bytes=62 * 2**20),
    )(queries.reshape(rows, width), key_states, value_states)
    return out[:, None, :]


def solution(mesh):
    return jax.shard_map(
        per_device,
        mesh=mesh,
        in_specs=(
            P("ctx", "head", None),
            P(("ctx", "head"), None, None),
            P(("ctx", "head"), None, None),
        ),
        out_specs=P("ctx", "head", None),
        check_vma=False,
    )
```

```python
import functools
import math

import jax
import jax.numpy as jnp
from jax import lax
from jax.experimental import pallas as pl
from jax.experimental.pallas import tpu as pltpu
from jax.sharding import PartitionSpec as P

MESH = pl.DeviceIdType.MESH
NEG = -1e30
BLOCKS = 16
QT = 256
XP, XM, X2, SIB, UP, SIB_XP, SIB_XM, SIB_X2, Y_X2, SIB_UP, Y = range(11)


def kernel(q_hbm, k_hbm, v_hbm, o_ref, q_ref, k_ref, v_ref, kv, stage, wide, qc, qh, oh, lh_out,
           help_o, help_l, m, l, acc, ss, rs, p1s, p1r, qsem, ssem, osem, isem):
    c = lax.axis_index("ctx")
    h = lax.axis_index("head")
    z, x, core = c // 8, (c // 2) % 4, c % 2
    group, lane = h // 4, h % 4
    rows = q_ref.shape[0]
    tiles = rows // QT

    def quarter(r):
        return (lane + r // 2) % 2 + 2 * ((lane // 2 + r % 2) % 2)

    def device(x_, z_, core_, lane_):
        return {"ctx": z_ * 8 + x_ * 2 + core_, "head": group * 4 + lane_}

    xp, xm, x2 = (x + 1) % 4, (x + 3) % 4, (x + 2) % 4
    to_xp, to_xm, to_x2 = (device(t, z, core, lane) for t in (xp, xm, x2))
    to_sib = device(x, z, 1 - core, lane)
    to_z = device(x, 1 - z, core, lane)
    to_mirror = device(3 - x, 1 - z, 1 - core, lane)
    to_y = device(x, z, core, quarter(2))
    to_group = [{"ctx": c, "head": ((group + d % 8) % 8) * 4 + quarter(d // 8)} for d in range(16)]

    barrier = pltpu.get_barrier_semaphore()
    partners = to_group[1:] + [to_y, to_xp, to_xm, to_x2, to_sib, to_z, to_mirror]
    for partner in partners:
        pl.semaphore_signal(barrier, inc=1, device_id=partner, device_id_type=MESH)

    loads = [pltpu.make_async_copy(src, dst, isem.at[i])
             for i, (src, dst) in enumerate(((k_hbm, k_ref), (v_hbm, v_ref), (q_hbm, q_ref)))]
    for copy in loads:
        copy.start()
    loads[0].wait()
    loads[1].wait()

    for ref, first in ((k_ref, 0), (v_ref, 32)):
        wide[...] = ref[...].astype(jnp.float32).reshape(wide.shape)
        for g in range(8):
            stage[g, first:first + 32] = wide[pl.ds(g, 32, stride=8), :].astype(jnp.bfloat16)
    kv[c, lane, group] = stage[group]

    scale = math.log2(math.e) / math.sqrt(q_ref.shape[1])

    def split_scaled(job, src):
        def one(i, _):
            r = pl.ds(pl.multiple_of(i * QT, QT), QT)
            scaled = src[r].astype(jnp.float32) * scale
            high = scaled.astype(jnp.bfloat16)
            qc[job, r, :128] = high
            qc[job, r, 128:] = (scaled - high.astype(jnp.float32)).astype(jnp.bfloat16)
            return 0
        lax.fori_loop(0, tiles, one, 0)

    loads[2].wait()
    split_scaled(0, q_ref)
    m[...] = jnp.full(m.shape, NEG, jnp.float32)
    l[...] = jnp.zeros(l.shape, jnp.float32)
    acc[...] = jnp.zeros(acc.shape, jnp.float32)

    pl.semaphore_wait(barrier, len(partners))

    def remote(src, dst, send, recv, to):
        return pltpu.make_async_remote_copy(
            src_ref=src, dst_ref=dst, send_sem=send, recv_sem=recv, device_id=to, device_id_type=MESH)

    def scatter(d):
        return remote(stage.at[(group + d % 8) % 8], kv.at[c, lane, group], p1s.at[d], p1r.at[d], to_group[d])

    for d in (4, 3, 5, 2, 6, 1, 7, 12, 11, 13, 10, 14, 9, 15, 8):
        scatter(d).start()
    query_copy = remote(q_ref, qh, qsem.at[0], qsem.at[1], to_mirror)
    is_late = z == 1
    is_early = z == 0

    pl.when(is_late & (x > 0))(query_copy.start)

    def piece(kind, r, block, to):
        q = quarter(r)
        return remote(kv.at[block, q], kv.at[block, q], ss.at[kind, r], rs.at[block, q], to)

    def landed(r, block):
        piece(0, r, block, to_sib).wait_recv()

    def from_chip(x_):
        return 2 * x_ + 8 * z * (x_ < x).astype(jnp.int32)

    own_up = 2 * x + core
    own_goes = {XP: x < 3, XM: x < 2 - z, X2: x < 3 - z}
    up_goes = {XP: is_late & (x == 3), XM: is_late & (x > 0), X2: is_late & (x > 1)}
    has_xp = is_late | (x == 0) | (x == 3)
    has_xm = is_late | (x > 0)
    has_x2 = is_late | (x != 1)
    helps = is_early & (x < 3)
    helped = is_late & (x > 0)
    targets = {XP: to_xp, XM: to_xm, X2: to_x2}

    def kinds_x(direct):
        return (XP, XM, X2) if direct else (XP, XM)

    def own_quarter(r, direct, first=False):
        if not first:
            landed(r, c)
        @pl.when(z == 0)
        def _():
            piece(UP, r, c, to_z).start()

        for kind in kinds_x(direct):
            @pl.when(own_goes[kind])
            def _(kind=kind):
                piece(kind, r, c, targets[kind]).start()

        piece(SIB, r, c, to_sib).start()

    def up_quarter(r, direct):
        @pl.when(is_late)
        def _():
            landed(r, own_up)
            for kind in kinds_x(direct):
                @pl.when(up_goes[kind])
                def _(kind=kind):
                    piece(kind, r, own_up, targets[kind]).start()
            piece(SIB_UP, r, own_up, to_sib).start()

    def x_quarters(r):
        def take(kind, source):
            landed(r, from_chip(source) + core)
            piece(kind, r, from_chip(source) + core, to_sib).start()

        pl.when(has_xp)(lambda: take(SIB_XP, xp))
        pl.when(has_xm)(lambda: take(SIB_XM, xm))

    def x2_quarter(r, direct):
        @pl.when(has_x2)
        def _():
            block = from_chip(x2) + core
            landed(r, block)
            if direct:
                piece(Y_X2, r, block, to_y).start()
            piece(SIB_X2, r, block, to_sib).start()

    def sib_own(r):
        landed(r, c + 1 - 2 * core)

    def sib_up(r):
        landed(r, own_up + 1 - 2 * core)

    def sib_x(r):
        @pl.when(has_xp)
        def _():
            landed(r, from_chip(xp) + 1 - core)

        @pl.when(has_xm)
        def _():
            landed(r, from_chip(xm) + 1 - core)

    def sib_x2(r):
        @pl.when(has_x2)
        def _():
            landed(r, from_chip(x2) + 1 - core)

    def attend(job, parts):
        scores = []
        for tile, (keys, values, mask) in enumerate(parts):
            at = slice(tile * QT, (tile + 1) * QT)
            score = lax.dot_general(qc[job, at], jnp.concatenate([keys, keys], axis=1),
                                    (((1,), (1,)), ((), ())), preferred_element_type=jnp.float32)
            scores.append(score if mask is None else jnp.where(mask, score, NEG))
        rounded, shrinks = [], []
        for tile, score in enumerate(scores):
            at = slice(tile * QT, (tile + 1) * QT)
            before = m[job, at]
            now = jnp.maximum(before, jnp.max(score, axis=1, keepdims=True))
            m[job, at] = now
            shrinks.append(jnp.exp2(before - now))
            across = jnp.concatenate([now] * (score.shape[1] // 128), axis=1)
            rounded.append(jnp.exp2(score - across).astype(jnp.bfloat16))
        for tile, (_, values, _) in enumerate(parts):
            at = slice(tile * QT, (tile + 1) * QT)
            mixed = jnp.dot(rounded[tile], jnp.concatenate([values, jnp.ones_like(values)], axis=1),
                            preferred_element_type=jnp.float32)
            acc[job, at] = acc[job, at] * shrinks[tile] + mixed[:, :128]
            l[job, at] = l[job, at] * shrinks[tile] + mixed[:, 128:]

    def load(blocks, half, first, count):
        parts = [(b, quarter(2 * half + i)) for b in blocks for i in range(2)]
        def side(at):
            return jnp.concatenate(
                [kv[b, q, pl.ds(first, count), at:at + 32, :].reshape(count * 32, 128) for b, q in parts], axis=0)
        return side(0), side(32)

    def diagonal(half):
        parts = []
        for tile in range(tiles):
            count = 2 * (tile + 1)
            keys, values = load([c], half, 0, count)
            spot = lax.broadcasted_iota(jnp.int32, (1, count * 64), 1)
            which = jnp.where(spot < count * 32, quarter(2 * half), quarter(2 * half + 1))
            inner = spot % (count * 32)
            key_pos = (inner // 32) * 128 + which * 32 + inner % 32
            query_pos = tile * QT + lax.broadcasted_iota(jnp.int32, (QT, 1), 0)
            parts.append((keys, values, key_pos <= query_pos))
        attend(0, parts)

    def single(half):
        keys, values = load([2 * x], half, 0, 8)
        attend(0, [(keys, values, None)] * tiles)

    def by_x(a0, a1, a2, a3):
        return jnp.where(x == 0, a0, jnp.where(x == 1, a1, jnp.where(x == 2, a2, a3)))

    def by_step(i, a0, a1, a2):
        return jnp.where(i == 0, a0, jnp.where(i == 1, a1, a2))

    def pair(i, half):
        late_base = from_chip(by_step(i - 1, xp, xm, x2))
        late_a = jnp.where(i == 0, own_up, late_base)
        late_b = jnp.where(i == 0, 2 * x + jnp.where(core == 0, 1, 8), late_base + 1)
        chip_a = by_step(i - 1, by_x(0, 1, 1, 0), by_x(1, 0, 0, 2), by_x(2, 0, 0, 1))
        job_a = by_step(i - 1, by_x(1, 1, 0, 0), by_x(1, 0, 0, 0), by_x(1, 1, 1, 0))
        chip_b = by_step(i - 1, by_x(0, 1, 0, 0), by_x(1, 0, 1, 2), by_x(2, 0, 0, 1))
        job_b = by_step(i - 1, by_x(1, 1, 1, 0), by_x(1, 1, 0, 0), by_x(1, 0, 0, 0))
        early_a = 2 * jnp.where(half == 0, chip_a, chip_b)
        job = jnp.where(is_late, 0, jnp.where(half == 0, job_a, job_b))
        blocks = [jnp.where(is_late, late_a, early_a), jnp.where(is_late, late_b, early_a + 1)]
        keys, values = load(blocks, half, 0, 8)
        attend(job, [(keys, values, None)] * tiles)

    def exchange(r):
        q = quarter(r)
        return remote(kv.at[c, q], kv.at[c, q], ss.at[Y, r], rs.at[c, q], to_y)

    for r, pieces in ((0, range(1, 8)), (1, range(8, 16))):
        for d in pieces:
            scatter(d).wait_recv()
        exchange(r).start()
        own_quarter(r, True, True)

    eye = (lax.broadcasted_iota(jnp.int32, (128, 128), 0) == lax.broadcasted_iota(jnp.int32, (128, 128), 1))
    log_copy = remote(lh_out, help_l, ssem.at[0], ssem.at[1], to_mirror)
    part_copies = [remote(oh.at[pl.ds(i * QT, QT)], help_o.at[pl.ds(i * QT, QT)], osem.at[i], osem.at[tiles + i], to_mirror)
                   for i in range(tiles)]

    def send_part():
        for i in range(rows // 128):
            at = slice(i * 128, (i + 1) * 128)
            log = m[1, at] + jnp.log2(l[1, at])
            lh_out[i:i + 1] = jnp.sum(jnp.where(eye, log, 0.0), axis=0, keepdims=True)
        log_copy.start()
        for i, copy in enumerate(part_copies):
            at = slice(i * QT, (i + 1) * QT)
            oh[at] = (acc[1, at] / l[1, at]).astype(jnp.bfloat16)
            copy.start()

    def both(half, _):
        first = half == 0
        r0, r1 = 2 * half, 2 * half + 1

        def one(i, _):
            @pl.when(jnp.where(is_early & (half == 1), i == 4, i == 0))
            def _():
                diagonal(half)

            @pl.when(first & (i == 0))
            def _():
                own_quarter(2, False)
                up_quarter(0, True)
                pl.when(is_early)(lambda: x_quarters(0))
                own_quarter(3, False)
                up_quarter(1, True)
                pl.when(is_early)(lambda: x2_quarter(0, True))

                @pl.when(helps)
                def _():
                    query_copy.wait_recv()
                    split_scaled(1, qh)

            @pl.when((half == 1) & (i == 0))
            def _():
                x2_quarter(2, False)
                x_quarters(3)
                x2_quarter(3, False)

            @pl.when(i == 0)
            def _():
                sib_own(r0)
                sib_own(r1)

                @pl.when(is_late)
                def _():
                    sib_up(r0)
                    sib_up(r1)

            @pl.when(first & (i == 1))
            def _():
                up_quarter(2, False)

                @pl.when(is_late)
                def _():
                    x_quarters(0)
                    x2_quarter(0, True)
                x_quarters(1)
                up_quarter(3, False)
                x2_quarter(1, True)

            @pl.when(i == jnp.where(is_early & (x < 2), 2, 1))
            def _():
                sib_x(r0)
                sib_x(r1)

            @pl.when(first & (i == 2))
            def _():
                x_quarters(2)

            @pl.when(i == jnp.where(is_late | (x != 2), 3, jnp.where(first, 2, 1)))
            def _():
                sib_x2(r0)
                sib_x2(r1)

            @pl.when((core == 1) & (i == jnp.where(is_early & (half == 1), 4, 0)))
            def _():
                single(half)

            @pl.when((i < 4) & (is_late | (i > 0)))
            def _():
                pair(i, half)

            @pl.when(helps & (half == 1) & (i == 3 - x))
            def _():
                send_part()
            return 0
        lax.fori_loop(0, 5, one, 0)
        return 0

    lax.fori_loop(0, 2, both, 0)

    @pl.when(jnp.logical_not(helped))
    def _():
        o_ref[...] = (acc[0] / l[0]).astype(jnp.bfloat16)

    @pl.when(helped)
    def _():
        log_copy.wait_recv()
        for i in range(rows // 128):
            if i % (QT // 128) == 0:
                part_copies[i * 128 // QT].wait_recv()
            at = slice(i * 128, (i + 1) * 128)
            log = jnp.sum(jnp.where(eye, help_l[i:i + 1], 0.0), axis=1, keepdims=True)
            mine = m[0, at]
            top = jnp.maximum(mine, log)
            w_mine, w_help = jnp.exp2(mine - top), jnp.exp2(log - top)
            total = l[0, at] * w_mine + w_help
            mixed = acc[0, at] * w_mine + help_o[at].astype(jnp.float32) * w_help
            o_ref[at] = (mixed / total).astype(jnp.bfloat16)
        query_copy.wait_send()

    @pl.when(helps)
    def _():
        for copy in [log_copy] + part_copies:
            copy.wait_send()
    for d in range(1, 16):
        scatter(d).wait_send()
    for r in range(4):
        sent = [(XP, own_goes[XP] | up_goes[XP]), (XM, own_goes[XM] | up_goes[XM]), (SIB, None), (SIB_XP, has_xp),
                (SIB_XM, has_xm), (SIB_X2, has_x2), (UP, is_early), (SIB_UP, is_late)]
        if r < 2:
            sent += [(X2, own_goes[X2] | up_goes[X2]), (Y_X2, has_x2), (Y, None)]
        for kind, when in sent:
            wait = piece(kind, r, c, to_sib).wait_send
            if when is None:
                wait()
            else:
                pl.when(when)(wait)


def per_device(queries, key_states, value_states):
    rows, _, width = queries.shape
    f32, bf16 = jnp.float32, jnp.bfloat16
    dma = pltpu.SemaphoreType.DMA
    out = pl.pallas_call(
        kernel,
        out_shape=jax.ShapeDtypeStruct((rows, width), bf16),
        in_specs=[pl.BlockSpec(memory_space=pltpu.HBM)] * 3,
        out_specs=pl.BlockSpec(memory_space=pltpu.VMEM),
        scratch_shapes=[
            pltpu.VMEM((rows, width), bf16),
            pltpu.VMEM(key_states.shape, bf16),
            pltpu.VMEM(value_states.shape, bf16),
            pltpu.VMEM((BLOCKS, 4, 8, 64, width), bf16),
            pltpu.VMEM((8, 64, width), bf16),
            pltpu.VMEM((256, width), f32),
            pltpu.VMEM((2, rows, 2 * width), bf16),
            pltpu.VMEM((rows, width), bf16),
            pltpu.VMEM((rows, width), bf16),
            pltpu.VMEM((8, 128), f32),
            pltpu.VMEM((rows, width), bf16),
            pltpu.VMEM((8, 128), f32),
            pltpu.VMEM((2, rows, width), f32),
            pltpu.VMEM((2, rows, width), f32),
            pltpu.VMEM((2, rows, width), f32),
            dma((11, 4)),
            dma((BLOCKS, 4)),
            dma((16,)),
            dma((16,)),
            dma((2,)),
            dma((2,)),
            dma((8,)),
            dma((3,)),
        ],
        name="folded_attention",
        cost_estimate=pl.CostEstimate(flops=4 * 128 * 8 * 1024 * 1024, bytes_accessed=2**20, transcendentals=2**23),
        compiler_params=pltpu.CompilerParams(
            collective_id=0, has_side_effects=True, vmem_limit_bytes=62 * 2**20),
    )(queries.reshape(rows, width), key_states, value_states)
    return out[:, None, :]


def solution(mesh):
    return jax.shard_map(
        per_device,
        mesh=mesh,
        in_specs=(
            P("ctx", "head", None),
            P(("ctx", "head"), None, None),
            P(("ctx", "head"), None, None),
        ),
        out_specs=P("ctx", "head", None),
        check_vma=False,
    )
```
